32 devices in a mesh: ctx: 16 (over z, y, core), head: 2 (over x).
Axes of the slice: x: 2, y: 2, z: 4, core: 2. Of those that a mesh axis runs over, the one named last changes fastest.
Arguments:
- doc_lengths: int32 [8], replicated, may hold values from 1 to 2304, 4096 in all
- queries: bfloat16 [2, 4096, 16384], P(None, 'ctx', 'head'), may hold values from -120 to 120
- rotated_key_rows: bfloat16 [2, 4096, 1024], P(None, ('ctx', 'head')), may hold values from -6 to 6
- value_row_matrix: bfloat16 [2, 4096, 1024], P(None, ('ctx', 'head')), may hold values from -6 to 6
Outputs:
- attended: bfloat16 [2, 4096, 16384], P(None, 'ctx', 'head')
The draws below stay inside these ranges and needn't reach their ends.
All inputs are finite; a program needn't handle non-finite values.
Results may differ from the reference program's by a relative error of at most 0.003.
Values may be sent and summed in bfloat16 or wider, within the bound.
A program may use at most 192 MiB of HBM per device.

```python
import math
import jax
import jax.numpy as jnp
import numpy as np
from jax import lax

QUERY_HEAD_COUNT = 128
VALUE_KEY_HEADS = 8
HEAD_SIZE = 128
TOK_DEV = 256
PACKED_TOKENS = 4096
NDOCS = 8
LONGEST = 2304


def shared_draw(key):
    base_angle = jax.random.fold_in(key, 31)
    unrotated_keys = jax.random.truncated_normal(jax.random.fold_in(base_angle, 1), -6.0, 6.0, (2, PACKED_TOKENS, VALUE_KEY_HEADS * HEAD_SIZE), jnp.float32)
    return unrotated_keys


def final_keys(key):
    unrotated_keys = shared_draw(key)
    return unrotated_keys


def draw_rotated_key_rows(key, part):
    return final_keys(key).astype(jnp.bfloat16)


def draw_queries(key, part):
    base_angle = jax.random.fold_in(key, 31)
    raw_queries = jax.random.truncated_normal(jax.random.fold_in(base_angle, 4), -6.0, 6.0, (2, PACKED_TOKENS, QUERY_HEAD_COUNT * HEAD_SIZE), jnp.float32)
    return raw_queries.astype(jnp.bfloat16)


def draw_value_row_matrix(key, part):
    base_angle = jax.random.fold_in(key, 57)
    random_noise = jax.random.truncated_normal(jax.random.fold_in(base_angle, 1), -3.5, 3.5, (2, PACKED_TOKENS, VALUE_KEY_HEADS * HEAD_SIZE), jnp.float32)
    rotary_angle = jax.random.uniform(jax.random.fold_in(base_angle, 2), (VALUE_KEY_HEADS * HEAD_SIZE,), jnp.float32, 0.0, 2.0 * math.pi)
    position = jnp.arange(PACKED_TOKENS, dtype=jnp.float32)
    trend = 2.0 * jnp.sin(2.0 * math.pi * position[:, None] / (3.0 * TOK_DEV) + rotary_angle[None, :])
    return (random_noise + trend[None, :, :]).astype(jnp.bfloat16)


def length_profile(number_of, total, limit, slope):
    portions = [(1 << 20) // math.isqrt(standing ** slope) + 1 for standing in range(2, number_of + 1)]
    rest, counts = total - limit - (number_of - 1), [1] * (number_of - 1)
    while rest > 0:
        free = [i for i in range(number_of - 1) if counts[i] < limit]
        pool, left = sum([portions[i] for i in free]), rest
        for i in free:
            addition = min(limit - counts[i], max(1, left * portions[i] // pool), rest)
            counts[i] = counts[i] + addition
            rest = rest - addition
    return np.array([limit] + counts)


def uneven(stream_key, count, total, bound, skew):
    if count == 2:
        one = jax.random.randint(stream_key, (), max(1, total - bound), min(bound, total - 1) + 1)
        return jnp.stack([one, total - one])
    sizes = jnp.asarray(length_profile(count, total, bound, skew), jnp.int32)
    twos = (count - 1) // 2
    giver, taker = sizes[1:1 + 2 * twos:2], sizes[2:2 + 2 * twos:2]
    margin = jnp.minimum(giver - 1, bound - taker)
    shifted = jax.random.randint(jax.random.fold_in(stream_key, 1), (twos,), 0, 1 << 20) % (margin + 1)
    sizes = sizes.at[1:1 + 2 * twos:2].set(giver - shifted).at[2:2 + 2 * twos:2].set(taker + shifted)
    return sizes[jax.random.permutation(jax.random.fold_in(stream_key, 2), count)]


def setup_inputs(seed: int = 0) -> dict:
    arg_keys = jax.random.split(jax.random.key(seed), 5)
    doc_lengths = uneven(arg_keys[0], NDOCS, PACKED_TOKENS, LONGEST, 2).astype(jnp.int32)
    queries = draw_queries(jax.random.fold_in(arg_keys[4], 71), 0)
    rotated_key_rows = draw_rotated_key_rows(jax.random.fold_in(arg_keys[4], 71), 0)
    value_row_matrix = draw_value_row_matrix(jax.random.fold_in(arg_keys[4], 71), 0)
    return dict(doc_lengths=doc_lengths, queries=queries, rotated_key_rows=rotated_key_rows, value_row_matrix=value_row_matrix)


NEG_FILL = -1.0e30


def doc_index(positions, doc_ends):
    return jnp.sum((positions[:, None] >= doc_ends[None, :]).astype(jnp.int32), axis=1)


def reference(doc_lengths, queries, rotated_key_rows, value_row_matrix):
    doc_ends = jnp.cumsum(doc_lengths).astype(jnp.int32)
    group_width = QUERY_HEAD_COUNT // VALUE_KEY_HEADS
    span = min(LONGEST + TOK_DEV, PACKED_TOKENS)
    block_count = PACKED_TOKENS // TOK_DEV
    query_tensor = queries.reshape(2, PACKED_TOKENS, VALUE_KEY_HEADS, group_width, HEAD_SIZE)
    key_tensor = rotated_key_rows.reshape(2, PACKED_TOKENS, VALUE_KEY_HEADS, HEAD_SIZE)
    value_tensor = value_row_matrix.reshape(2, PACKED_TOKENS, VALUE_KEY_HEADS, HEAD_SIZE)

    def one_block(block_index):
        query_start = (block_index * TOK_DEV).astype(jnp.int32)
        key_start = jnp.maximum(query_start + TOK_DEV - span, 0).astype(jnp.int32)
        query_block = lax.dynamic_slice_in_dim(query_tensor, query_start, TOK_DEV, 1)
        key_block = lax.dynamic_slice_in_dim(key_tensor, key_start, span, 1)
        value_block = lax.dynamic_slice_in_dim(value_tensor, key_start, span, 1)
        query_pos = query_start + jnp.arange(TOK_DEV, dtype=jnp.int32)
        key_pos = key_start + jnp.arange(span, dtype=jnp.int32)
        allowed = (doc_index(key_pos, doc_ends)[None, :] == doc_index(query_pos, doc_ends)[:, None]) & (key_pos[None, :] <= query_pos[:, None])

        def single_head(head_index):
            query_head = lax.dynamic_index_in_dim(query_block, head_index, 2, keepdims=False).astype(jnp.float32)
            key_head = lax.dynamic_index_in_dim(key_block, head_index, 2, keepdims=False).astype(jnp.float32)
            value_head = lax.dynamic_index_in_dim(value_block, head_index, 2, keepdims=False).astype(jnp.float32)
            scores = jnp.einsum("bqgd,bsd->bgqs", query_head, key_head) * (HEAD_SIZE ** -0.5)
            scores = jnp.where(allowed, scores, NEG_FILL)
            peak = jnp.max(scores, axis=-1, keepdims=True)
            probs = jnp.where(allowed, jnp.exp(scores - peak), 0.0)
            total = jnp.sum(probs, axis=-1)
            rounded = lax.optimization_barrier(probs.astype(jnp.bfloat16)).astype(jnp.float32)
            accum = jnp.einsum("bgqs,bsd->bgqd", rounded, value_head)
            return accum / total[..., None]

        head_outputs = lax.map(single_head, jnp.arange(VALUE_KEY_HEADS, dtype=jnp.int32))
        merged = jnp.transpose(head_outputs, (1, 3, 0, 2, 4)).reshape(2, TOK_DEV, QUERY_HEAD_COUNT * HEAD_SIZE)
        return merged.astype(jnp.bfloat16)

    blocks = lax.map(one_block, jnp.arange(block_count, dtype=jnp.int32))
    return jnp.transpose(blocks, (1, 0, 2, 3)).reshape(2, PACKED_TOKENS, QUERY_HEAD_COUNT * HEAD_SIZE)
```

```python
import functools

import jax
import jax.numpy as jnp
from jax import lax
from jax.experimental import pallas as pl
from jax.experimental.pallas import tpu as pltpu
from jax.sharding import PartitionSpec as P

HEAD_SIZE = 128
NEG_FILL = -1e30
LOG2E = 1.4426950408889634
ONES_ROWS = 16
HEADS_STEP = 4


def attend_kernel(bounds, queries, keys, values, starts, *rest):
    out, q_t, peak, acc = rest[-4:]
    tokens = queries.shape[0]
    heads = queries.shape[1] // HEAD_SIZE
    scale = HEAD_SIZE ** -0.5 * LOG2E
    own, full_low, low = bounds[0], bounds[1], bounds[2]

    for h in range(heads):
        q_t[h] = queries[:, h * HEAD_SIZE:(h + 1) * HEAD_SIZE].T

    def visit(block, masked, first):
        k = keys[block]
        v_t = values[block].T
        v_ext = jnp.concatenate([v_t, jnp.ones((ONES_ROWS, tokens), v_t.dtype)], axis=0)
        if masked:
            shape = (tokens, tokens)
            key_pos = block * tokens + lax.broadcasted_iota(jnp.int32, shape, 0)
            query_pos = own * tokens + lax.broadcasted_iota(jnp.int32, shape, 1)
            allowed = (key_pos <= query_pos) & (key_pos >= starts[...])

        def score(h):
            return jnp.dot(k, q_t[h], preferred_element_type=jnp.float32)

        def group(g, carry):
            base = g * HEADS_STEP
            ahead = score(base)
            for i in range(HEADS_STEP):
                h = base + i
                s = ahead
                if i + 1 < HEADS_STEP:
                    ahead = score(h + 1)
                if masked:
                    s = jnp.where(allowed, s, NEG_FILL)
                top = jnp.max(s, axis=0, keepdims=True) * scale
                if first:
                    new = top
                else:
                    old = peak[h]
                    new = jnp.maximum(old, top)
                probs = jnp.exp2(s * scale - new).astype(jnp.bfloat16)
                part = jnp.dot(v_ext, probs, preferred_element_type=jnp.float32)
                if first:
                    acc[h] = part
                else:
                    acc[h] = acc[h] * jnp.exp2(old - new) + part
                peak[h] = new
            return carry

        lax.fori_loop(0, heads // HEADS_STEP, group, 0)

    visit(own, True, True)

    @pl.loop(0, own - full_low)
    def _(t):
        visit(own - 1 - t, False, False)

    @pl.loop(0, full_low - low)
    def _(t):
        visit(full_low - 1 - t, True, False)

    for h in range(heads):
        a = acc[h]
        mixed = a[:HEAD_SIZE] / a[HEAD_SIZE:HEAD_SIZE + 1]
        out[:, h * HEAD_SIZE:(h + 1) * HEAD_SIZE] = mixed.T.astype(out.dtype)


def attend(model, bounds, queries, gathered, starts, previous):
    models, tokens, width = queries.shape
    blocks, _, _, kv_width = gathered.shape
    kv_heads = kv_width // HEAD_SIZE
    group = width // kv_heads
    heads = group // HEAD_SIZE
    in_specs = [
        pl.BlockSpec((None, tokens, group), lambda g, b: (model, 0, g)),
        pl.BlockSpec((blocks, None, tokens, HEAD_SIZE), lambda g, b: (0, 0, 0, g)),
        pl.BlockSpec((blocks, None, tokens, HEAD_SIZE), lambda g, b: (0, 1, 0, g)),
        pl.BlockSpec((1, tokens), lambda g, b: (0, 0)),
    ]
    args = [bounds, queries, gathered, gathered, starts]
    aliases = {}
    if previous is not None:
        in_specs.append(pl.BlockSpec(memory_space=pl.ANY))
        aliases = {len(args): 0}
        args.append(previous)
    flops = 4 * tokens * width * tokens * 6
    return pl.pallas_call(
        attend_kernel,
        out_shape=jax.ShapeDtypeStruct(queries.shape, queries.dtype),
        grid_spec=pltpu.PrefetchScalarGridSpec(
            num_scalar_prefetch=1,
            grid=(kv_heads,),
            in_specs=in_specs,
            out_specs=pl.BlockSpec((None, tokens, group), lambda g, b: (model, 0, g)),
            scratch_shapes=[
                pltpu.VMEM((heads, HEAD_SIZE, tokens), jnp.bfloat16),
                pltpu.VMEM((heads, 1, tokens), jnp.float32),
                pltpu.VMEM((heads, HEAD_SIZE + ONES_ROWS, tokens), jnp.float32),
            ],
        ),
        input_output_aliases=aliases,
        cost_estimate=pl.CostEstimate(flops=flops, bytes_accessed=2 * tokens * width * 4, transcendentals=0),
        compiler_params=pltpu.CompilerParams(vmem_limit_bytes=40 * 1024 * 1024),
    )(*args)


def shards(doc_lengths, queries, rotated_key_rows, value_row_matrix):
    models, tokens, _ = queries.shape
    own = lax.axis_index("ctx").astype(jnp.int32)
    doc_ends = jnp.cumsum(doc_lengths).astype(jnp.int32)
    pos = own * tokens + jnp.arange(tokens, dtype=jnp.int32)
    starts = jnp.max(jnp.where(doc_ends[None, :] <= pos[:, None], doc_ends[None, :], 0), axis=1)
    low = starts[0] // tokens
    full_low = jnp.minimum((starts[-1] + tokens - 1) // tokens, own)
    bounds = jnp.stack([own, full_low, low]).astype(jnp.int32)
    starts = starts[None, :]

    both = jnp.stack([rotated_key_rows, value_row_matrix], axis=1)
    local = lax.all_to_all(both, "head", split_axis=3, concat_axis=2, tiled=True)
    out = None
    for model in range(models):
        gathered = lax.all_gather(local[model], "ctx", axis=0)
        out = attend(model, bounds, queries, gathered, starts, out)
    return out


def solution(mesh):
    placed = (
        P(),
        P(None, "ctx", "head"),
        P(None, ("ctx", "head"), None),
        P(None, ("ctx", "head"), None),
    )
    return jax.shard_map(
        shards, mesh=mesh, in_specs=placed, out_specs=P(None, "ctx", "head"), check_vma=False
    )
```

```python
import functools

import jax
import jax.numpy as jnp
from jax import lax
from jax.experimental import pallas as pl
from jax.experimental.pallas import tpu as pltpu
from jax.sharding import PartitionSpec as P

HEAD_SIZE = 128
NEG_FILL = -1e30
LOG2E = 1.4426950408889634
ONES_ROWS = 16
HEADS_STEP = 8


def attend_kernel(bounds, queries, keys, values, starts, *rest):
    out, q_t, peak, acc = rest[-4:]
    tokens = queries.shape[0]
    heads = queries.shape[1] // HEAD_SIZE
    scale = HEAD_SIZE ** -0.5 * LOG2E
    own, full_low, low = bounds[0], bounds[1], bounds[2]

    for h in range(heads):
        q_t[h] = queries[:, h * HEAD_SIZE:(h + 1) * HEAD_SIZE].T

    def visit(block, span, masked, first):
        rows = span * tokens
        if span == 1:
            k, v = keys[block], values[block]
        else:
            k = keys[pl.ds(block, span)].reshape(rows, HEAD_SIZE)
            v = values[pl.ds(block, span)].reshape(rows, HEAD_SIZE)
        v_ext = jnp.concatenate([v.T, jnp.ones((ONES_ROWS, rows), v.dtype)], axis=0)
        if masked:
            shape = (rows, tokens)
            key_pos = block * tokens + lax.broadcasted_iota(jnp.int32, shape, 0)
            query_pos = own * tokens + lax.broadcasted_iota(jnp.int32, shape, 1)
            allowed = (key_pos <= query_pos) & (key_pos >= starts[...])

        def score(h):
            return jnp.dot(k, q_t[h], preferred_element_type=jnp.float32)

        def group(g, carry):
            base = g * HEADS_STEP
            ahead = score(base)
            for i in range(HEADS_STEP):
                h = base + i
                s = ahead
                if i + 1 < HEADS_STEP:
                    ahead = score(h + 1)
                if masked:
                    s = jnp.where(allowed, s, NEG_FILL)
                top = jnp.max(s, axis=0, keepdims=True) * scale
                if first:
                    new = top
                else:
                    old = peak[h]
                    new = jnp.maximum(old, top)
                probs = jnp.exp2(s * scale - new).astype(jnp.bfloat16)
                part = jnp.dot(v_ext, probs, preferred_element_type=jnp.float32)
                if first:
                    acc[h] = part
                else:
                    acc[h] = acc[h] * jnp.exp2(old - new) + part
                peak[h] = new
            return carry

        lax.fori_loop(0, heads // HEADS_STEP, group, 0)

    visit(own, 1, True, True)
    full = own - full_low

    @pl.loop(0, full // 2)
    def _(t):
        visit(own - 2 - 2 * t, 2, False, False)

    @pl.loop(0, full % 2)
    def _(t):
        visit(full_low, 1, False, False)

    @pl.loop(0, full_low - low)
    def _(t):
        visit(full_low - 1 - t, 1, True, False)

    for h in range(heads):
        a = acc[h]
        mixed = a[:HEAD_SIZE] / a[HEAD_SIZE:HEAD_SIZE + 1]
        out[:, h * HEAD_SIZE:(h + 1) * HEAD_SIZE] = mixed.T.astype(out.dtype)


def attend(model, place, kv_heads, bounds, queries, gathered, starts, previous):
    models, tokens, width = queries.shape
    blocks = gathered.shape[0]
    group = width // kv_heads
    heads = group // HEAD_SIZE
    in_specs = [
        pl.BlockSpec((None, tokens, group), lambda g, b: (model, 0, place)),
        pl.BlockSpec((blocks, None, tokens, HEAD_SIZE), lambda g, b: (0, 0, 0, 0)),
        pl.BlockSpec((blocks, None, tokens, HEAD_SIZE), lambda g, b: (0, 1, 0, 0)),
        pl.BlockSpec((1, tokens), lambda g, b: (0, 0)),
    ]
    args = [bounds, queries, gathered, gathered, starts]
    aliases = {}
    if previous is not None:
        in_specs.append(pl.BlockSpec(memory_space=pl.ANY))
        aliases = {len(args): 0}
        args.append(previous)
    flops = 4 * tokens * group * tokens * 12
    return pl.pallas_call(
        attend_kernel,
        out_shape=jax.ShapeDtypeStruct(queries.shape, queries.dtype),
        grid_spec=pltpu.PrefetchScalarGridSpec(
            num_scalar_prefetch=1,
            grid=(1,),
            in_specs=in_specs,
            out_specs=pl.BlockSpec((None, tokens, group), lambda g, b: (model, 0, place)),
            scratch_shapes=[
                pltpu.VMEM((heads, HEAD_SIZE, tokens), jnp.bfloat16),
                pltpu.VMEM((heads, 1, tokens), jnp.float32),
                pltpu.VMEM((heads, HEAD_SIZE + ONES_ROWS, tokens), jnp.float32),
            ],
        ),
        input_output_aliases=aliases,
        cost_estimate=pl.CostEstimate(flops=flops, bytes_accessed=4 * tokens * group, transcendentals=0),
        compiler_params=pltpu.CompilerParams(vmem_limit_bytes=56 * 1024 * 1024),
    )(*args)


def exchange(both, ranks):
    mine = lax.axis_index("head")
    kind, rows, features = both.shape
    width = features // ranks
    local = jnp.zeros((kind, rows * ranks, width), both.dtype)
    for step in range(ranks):
        piece = lax.dynamic_slice_in_dim(both, (mine + step) % ranks * width, width, 2)
        if step:
            piece = lax.ppermute(piece, "head", [(i, (i + step) % ranks) for i in range(ranks)])
        source = (mine + ranks - step) % ranks
        local = lax.dynamic_update_slice_in_dim(local, piece, source * rows, 1)
    return local


def shards(ranks, doc_lengths, queries, rotated_key_rows, value_row_matrix):
    models, tokens, _ = queries.shape
    own = lax.axis_index("ctx").astype(jnp.int32)
    doc_ends = jnp.cumsum(doc_lengths).astype(jnp.int32)
    pos = own * tokens + jnp.arange(tokens, dtype=jnp.int32)
    starts = jnp.max(jnp.where(doc_ends[None, :] <= pos[:, None], doc_ends[None, :], 0), axis=1)
    low = starts[0] // tokens
    full_low = jnp.minimum((starts[-1] + tokens - 1) // tokens, own)
    bounds = jnp.stack([own, full_low, low]).astype(jnp.int32)
    starts = starts[None, :]

    kv_heads = rotated_key_rows.shape[2] // (ranks * HEAD_SIZE)
    out = None
    for model in range(models):
        local = exchange(jnp.stack([rotated_key_rows[model], value_row_matrix[model]]), ranks)
        for place in range(kv_heads):
            part = local[:, :, place * HEAD_SIZE:(place + 1) * HEAD_SIZE]
            gathered = lax.all_gather(part, "ctx", axis=0)
            out = attend(model, place, kv_heads, bounds, queries, gathered, starts, out)
    return out


def solution(mesh):
    placed = (
        P(),
        P(None, "ctx", "head"),
        P(None, ("ctx", "head"), None),
        P(None, ("ctx", "head"), None),
    )
    return jax.shard_map(
        functools.partial(shards, mesh.shape["head"]), mesh=mesh, in_specs=placed, out_specs=P(None, "ctx", "head"), check_vma=False
    )
```

```python
import functools

import jax
import jax.numpy as jnp
from jax import lax
from jax.experimental import pallas as pl
from jax.experimental.pallas import tpu as pltpu
from jax.sharding import PartitionSpec as P

HEAD_SIZE = 128
NEG_FILL = -1e30
LOG2E = 1.4426950408889634
ONES_ROWS = 16
HEADS_STEP = 4


def attend_kernel(bounds, queries, keys, values, starts, *rest):
    out, q_t, peak, acc = rest[-4:]
    tokens = queries.shape[0]
    heads = queries.shape[1] // HEAD_SIZE
    scale = HEAD_SIZE ** -0.5 * LOG2E
    own, full_low, low = bounds[0], bounds[1], bounds[2]

    for h in range(heads):
        q_t[h] = queries[:, h * HEAD_SIZE:(h + 1) * HEAD_SIZE].T

    def visit(block, span, masked, first):
        rows = span * tokens
        if span == 1:
            k, v = keys[block], values[block]
        else:
            k = keys[pl.ds(block, span)].reshape(rows, HEAD_SIZE)
            v = values[pl.ds(block, span)].reshape(rows, HEAD_SIZE)
        v_ext = jnp.concatenate([v.T, jnp.ones((ONES_ROWS, rows), v.dtype)], axis=0)
        if masked:
            shape = (rows, tokens)
            key_pos = block * tokens + lax.broadcasted_iota(jnp.int32, shape, 0)
            query_pos = own * tokens + lax.broadcasted_iota(jnp.int32, shape, 1)
            allowed = (key_pos <= query_pos) & (key_pos >= starts[...])

        def score(h):
            return jnp.dot(k, q_t[h], preferred_element_type=jnp.float32)

        def group(g, carry):
            base = g * HEADS_STEP
            ahead = score(base)
            for i in range(HEADS_STEP):
                h = base + i
                s = ahead
                if i + 1 < HEADS_STEP:
                    ahead = score(h + 1)
                if masked:
                    s = jnp.where(allowed, s, NEG_FILL)
                top = jnp.max(s, axis=0, keepdims=True) * scale
                if first:
                    new = top
                else:
                    old = peak[h]
                    new = jnp.maximum(old, top)
                probs = jnp.exp2(s * scale - new).astype(jnp.bfloat16)
                part = jnp.dot(v_ext, probs, preferred_element_type=jnp.float32)
                if first:
                    acc[h] = part
                else:
                    acc[h] = acc[h] * jnp.exp2(old - new) + part
                peak[h] = new
            return carry

        lax.fori_loop(0, heads // HEADS_STEP, group, 0)

    visit(own, 1, True, True)
    @pl.loop(0, own - full_low)
    def _(t):
        visit(own - 1 - t, 1, False, False)

    @pl.loop(0, full_low - low)
    def _(t):
        visit(full_low - 1 - t, 1, True, False)

    for h in range(heads):
        a = acc[h]
        mixed = a[:HEAD_SIZE] / a[HEAD_SIZE:HEAD_SIZE + 1]
        out[:, h * HEAD_SIZE:(h + 1) * HEAD_SIZE] = mixed.T.astype(out.dtype)


def attend(model, bounds, queries, gathered, starts, previous):
    models, tokens, width = queries.shape
    blocks = gathered.shape[0]
    kv_heads = gathered.shape[3] // HEAD_SIZE
    group = width // kv_heads
    heads = group // HEAD_SIZE
    in_specs = [
        pl.BlockSpec((None, tokens, group), lambda g, b: (model, 0, g)),
        pl.BlockSpec((blocks, None, tokens, HEAD_SIZE), lambda g, b: (0, 0, 0, g)),
        pl.BlockSpec((blocks, None, tokens, HEAD_SIZE), lambda g, b: (0, 1, 0, g)),
        pl.BlockSpec((1, tokens), lambda g, b: (0, 0)),
    ]
    args = [bounds, queries, gathered, gathered, starts]
    aliases = {}
    if previous is not None:
        in_specs.append(pl.BlockSpec(memory_space=pl.ANY))
        aliases = {len(args): 0}
        args.append(previous)
    flops = 4 * tokens * width * tokens * 12
    return pl.pallas_call(
        attend_kernel,
        out_shape=jax.ShapeDtypeStruct(queries.shape, queries.dtype),
        grid_spec=pltpu.PrefetchScalarGridSpec(
            num_scalar_prefetch=1,
            grid=(kv_heads,),
            in_specs=in_specs,
            out_specs=pl.BlockSpec((None, tokens, group), lambda g, b: (model, 0, g)),
            scratch_shapes=[
                pltpu.VMEM((heads, HEAD_SIZE, tokens), jnp.bfloat16),
                pltpu.VMEM((heads, 1, tokens), jnp.float32),
                pltpu.VMEM((heads, HEAD_SIZE + ONES_ROWS, tokens), jnp.float32),
            ],
        ),
        input_output_aliases=aliases,
        cost_estimate=pl.CostEstimate(flops=flops, bytes_accessed=4 * tokens * width, transcendentals=0),
        compiler_params=pltpu.CompilerParams(vmem_limit_bytes=56 * 1024 * 1024),
    )(*args)


def exchange(both, ranks):
    mine = lax.axis_index("head")
    kind, rows, features = both.shape
    width = features // ranks
    local = jnp.zeros((kind, rows * ranks, width), both.dtype)
    for step in range(ranks):
        piece = lax.dynamic_slice_in_dim(both, (mine + step) % ranks * width, width, 2)
        if step:
            piece = lax.ppermute(piece, "head", [(i, (i + step) % ranks) for i in range(ranks)])
        source = (mine + ranks - step) % ranks
        local = lax.dynamic_update_slice_in_dim(local, piece, source * rows, 1)
    return local


def shards(ranks, doc_lengths, queries, rotated_key_rows, value_row_matrix):
    models, tokens, _ = queries.shape
    own = lax.axis_index("ctx").astype(jnp.int32)
    doc_ends = jnp.cumsum(doc_lengths).astype(jnp.int32)
    pos = own * tokens + jnp.arange(tokens, dtype=jnp.int32)
    starts = jnp.max(jnp.where(doc_ends[None, :] <= pos[:, None], doc_ends[None, :], 0), axis=1)
    low = starts[0] // tokens
    full_low = jnp.minimum((starts[-1] + tokens - 1) // tokens, own)
    bounds = jnp.stack([own, full_low, low]).astype(jnp.int32)
    starts = starts[None, :]

    out = None
    for model in range(models):
        local = exchange(jnp.stack([rotated_key_rows[model], value_row_matrix[model]]), ranks)
        gathered = lax.all_gather(local, "ctx", axis=0)
        out = attend(model, bounds, queries, gathered, starts, out)
    return out


def solution(mesh):
    placed = (
        P(),
        P(None, "ctx", "head"),
        P(None, ("ctx", "head"), None),
        P(None, ("ctx", "head"), None),
    )
    return jax.shard_map(
        functools.partial(shards, mesh.shape["head"]), mesh=mesh, in_specs=placed, out_specs=P(None, "ctx", "head"), check_vma=False
    )
```

```python
import functools

import jax
import jax.numpy as jnp
from jax import lax
from jax.experimental import pallas as pl
from jax.experimental.pallas import tpu as pltpu
from jax.sharding import PartitionSpec as P

HEAD_SIZE = 128
NEG_FILL = -1e30
LOG2E = 1.4426950408889634
ONES_ROWS = 16
HEADS_STEP = 8


def attend_kernel(bounds, queries, keys, values, starts, *rest):
    out, q_t, peak, acc = rest[-4:]
    tokens = queries.shape[0]
    heads = queries.shape[1] // HEAD_SIZE
    scale = HEAD_SIZE ** -0.5 * LOG2E
    own, full_low, low = bounds[0], bounds[1], bounds[2]

    for h in range(heads):
        q_t[h] = queries[:, h * HEAD_SIZE:(h + 1) * HEAD_SIZE].T

    def visit(block, span, masked, first):
        rows = span * tokens
        if span == 1:
            k, v = keys[block], values[block]
        else:
            k = keys[pl.ds(block, span)].reshape(rows, HEAD_SIZE)
            v = values[pl.ds(block, span)].reshape(rows, HEAD_SIZE)
        v_ext = jnp.concatenate([v.T, jnp.ones((ONES_ROWS, rows), v.dtype)], axis=0)
        if masked:
            shape = (rows, tokens)
            key_pos = block * tokens + lax.broadcasted_iota(jnp.int32, shape, 0)
            query_pos = own * tokens + lax.broadcasted_iota(jnp.int32, shape, 1)
            allowed = (key_pos <= query_pos) & (key_pos >= starts[...])

        def score(h):
            return jnp.dot(k, q_t[h], preferred_element_type=jnp.float32)

        def group(g, carry):
            base = g * HEADS_STEP
            ahead = score(base)
            for i in range(HEADS_STEP):
                h = base + i
                s = ahead
                if i + 1 < HEADS_STEP:
                    ahead = score(h + 1)
                if masked:
                    s = jnp.where(allowed, s, NEG_FILL)
                top = jnp.max(s, axis=0, keepdims=True) * scale
                if first:
                    new = top
                else:
                    old = peak[h]
                    new = jnp.maximum(old, top)
                probs = jnp.exp2(s * scale - new).astype(jnp.bfloat16)
                part = jnp.dot(v_ext, probs, preferred_element_type=jnp.float32)
                if first:
                    acc[h] = part
                else:
                    acc[h] = acc[h] * jnp.exp2(old - new) + part
                peak[h] = new
            return carry

        lax.fori_loop(0, heads // HEADS_STEP, group, 0)

    visit(own, 1, True, True)
    @pl.loop(0, own - full_low)
    def _(t):
        visit(own - 1 - t, 1, False, False)

    @pl.loop(0, full_low - low)
    def _(t):
        visit(full_low - 1 - t, 1, True, False)

    for h in range(heads):
        a = acc[h]
        mixed = a[:HEAD_SIZE] / a[HEAD_SIZE:HEAD_SIZE + 1]
        out[:, h * HEAD_SIZE:(h + 1) * HEAD_SIZE] = mixed.T.astype(out.dtype)


def attend(model, bounds, queries, gathered, starts, previous):
    models, tokens, width = queries.shape
    blocks = gathered.shape[0]
    kv_heads = gathered.shape[3] // HEAD_SIZE
    group = width // kv_heads
    heads = group // HEAD_SIZE
    in_specs = [
        pl.BlockSpec((None, tokens, group), lambda g, b: (model, 0, g)),
        pl.BlockSpec((blocks, None, tokens, HEAD_SIZE), lambda g, b: (0, 0, 0, g)),
        pl.BlockSpec((blocks, None, tokens, HEAD_SIZE), lambda g, b: (0, 1, 0, g)),
        pl.BlockSpec((1, tokens), lambda g, b: (0, 0)),
    ]
    args = [bounds, queries, gathered, gathered, starts]
    aliases = {}
    if previous is not None:
        in_specs.append(pl.BlockSpec(memory_space=pl.ANY))
        aliases = {len(args): 0}
        args.append(previous)
    flops = 4 * tokens * width * tokens * 12
    return pl.pallas_call(
        attend_kernel,
        out_shape=jax.ShapeDtypeStruct(queries.shape, queries.dtype),
        grid_spec=pltpu.PrefetchScalarGridSpec(
            num_scalar_prefetch=1,
            grid=(kv_heads,),
            in_specs=in_specs,
            out_specs=pl.BlockSpec((None, tokens, group), lambda g, b: (model, 0, g)),
            scratch_shapes=[
                pltpu.VMEM((heads, HEAD_SIZE, tokens), jnp.bfloat16),
                pltpu.VMEM((heads, 1, tokens), jnp.float32),
                pltpu.VMEM((heads, HEAD_SIZE + ONES_ROWS, tokens), jnp.float32),
            ],
        ),
        input_output_aliases=aliases,
        cost_estimate=pl.CostEstimate(flops=flops, bytes_accessed=4 * tokens * width, transcendentals=0),
        compiler_params=pltpu.CompilerParams(vmem_limit_bytes=56 * 1024 * 1024),
    )(*args)


def exchange(both, ranks):
    mine = lax.axis_index("head")
    kind, rows, features = both.shape
    width = features // ranks
    local = jnp.zeros((kind, rows * ranks, width), both.dtype)
    for step in range(ranks):
        piece = lax.dynamic_slice_in_dim(both, (mine + step) % ranks * width, width, 2)
        if step:
            piece = lax.ppermute(piece, "head", [(i, (i + step) % ranks) for i in range(ranks)])
        source = (mine + ranks - step) % ranks
        local = lax.dynamic_update_slice_in_dim(local, piece, source * rows, 1)
    return local


def shards(ranks, doc_lengths, queries, rotated_key_rows, value_row_matrix):
    models, tokens, _ = queries.shape
    own = lax.axis_index("ctx").astype(jnp.int32)
    doc_ends = jnp.cumsum(doc_lengths).astype(jnp.int32)
    pos = own * tokens + jnp.arange(tokens, dtype=jnp.int32)
    starts = jnp.max(jnp.where(doc_ends[None, :] <= pos[:, None], doc_ends[None, :], 0), axis=1)
    low = starts[0] // tokens
    full_low = jnp.minimum((starts[-1] + tokens - 1) // tokens, own)
    bounds = jnp.stack([own, full_low, low]).astype(jnp.int32)
    starts = starts[None, :]

    out = None
    for model in range(models):
        local = exchange(jnp.stack([rotated_key_rows[model], value_row_matrix[model]]), ranks)
        gathered = lax.all_gather(local, "ctx", axis=0)
        out = attend(model, bounds, queries, gathered, starts, out)
    return out


def solution(mesh):
    placed = (
        P(),
        P(None, "ctx", "head"),
        P(None, ("ctx", "head"), None),
        P(None, ("ctx", "head"), None),
    )
    return jax.shard_map(
        functools.partial(shards, mesh.shape["head"]), mesh=mesh, in_specs=placed, out_specs=P(None, "ctx", "head"), check_vma=False
    )
```
